32 devices in a mesh: req: 16 (over z, y, x), head: 2 (over core).
Axes of the slice: x: 2, y: 2, z: 4, core: 2. Of those that a mesh axis runs over, the one named last changes fastest.
Arguments:
- tokens: bfloat16 [32, 1024], P('req'), may hold values from -6 to 6
- self_keys: bfloat16 [32, 512, 1024], P('req', None, 'head'), may hold values from -240 to 240
- self_values: bfloat16 [32, 512, 1024], P('req', None, 'head'), may hold values from -6 to 6
- self_len: int32 [32], P('req'), may hold values from 1 to 512, as said below
- cross_keys: bfloat16 [32, 512, 1024], P('req', None, 'head'), may hold values from -240 to 240
- cross_values: bfloat16 [32, 512, 1024], P('req', None, 'head'), may hold values from -6 to 6
- cross_len: int32 [32], P('req'), may hold values from 1 to 512, as said below
- give_slot: int32 [16], P('req'), may hold values from 0 to 1
- w_query: bfloat16 [1024, 1024], P(None, 'head'), may hold values from -0.1875 to 0.1875
- w_key: bfloat16 [1024, 1024], P(None, 'head'), may hold values from -0.1875 to 0.1875
- w_value: bfloat16 [1024, 1024], P(None, 'head'), may hold values from -0.1875 to 0.1875
- w_out: bfloat16 [1024, 1024], P('head'), may hold values from -0.1875 to 0.1875
- w_cross_query: bfloat16 [1024, 1024], P(None, 'head'), may hold values from -0.1875 to 0.1875
- w_cross_out: bfloat16 [1024, 1024], P('head'), may hold values from -0.1875 to 0.1875
- w_up: bfloat16 [1024, 4096], P(None, 'head'), may hold values from -0.1875 to 0.1875
- w_down: bfloat16 [4096, 1024], P('head'), may hold values from -0.09375 to 0.09375
- gain_self: float32 [1024], replicated, may hold values from 0.1 to 1.9
- gain_cross: float32 [1024], replicated, may hold values from 0.1 to 1.9
- gain_final: float32 [1024], replicated, may hold values from 0.1 to 1.9
Outputs:
- decoded: bfloat16 [32, 1024], P('req')
- new_keys: bfloat16 [32, 1024], P('req', 'head')
- new_values: bfloat16 [32, 1024], P('req', 'head')
- moved_keys: bfloat16 [16, 512, 1024], P('req', None, 'head')
- moved_values: bfloat16 [16, 512, 1024], P('req', None, 'head')
The draws below stay inside these ranges and needn't reach their ends.
Inputs may be any that keep to these rules, and one draw needn't show every extreme that they name: `self_len`: each request fills at least one slot; some request fills all 512. `cross_len`: each request has at least one encoder position; some request has 512.
All inputs are finite; a program needn't handle non-finite values.
Results may differ from the reference program's by a relative error of at most 0.039.
Values may be sent and summed in bfloat16 or wider, within the bound.
A program may use at most 64 MiB of HBM per device.

```python
import jax
import jax.numpy as jnp
from jax import lax

D = 1024
HEADS = 16
HEAD_DIM = 64
FF = 4096
REQ_DEV = 2
S_MAX = 512
E_MAX = 512
REQUESTS = 32
MOVES = 16


def length_draw(key, count, most):
    first_key, second_key, third_key = jax.random.split(key, 3)
    one = jax.random.randint(first_key, (count,), 1, most + 1)
    two = jax.random.randint(second_key, (count,), 1, most + 1)
    lengths = jnp.minimum(one, two)
    spot = jax.random.randint(third_key, (), 0, count)
    return jnp.where(jnp.arange(count) == spot, most, lengths).astype(jnp.int32)


def key_draw(key, count, span):
    base_key = jax.random.fold_in(key, 0)
    values = jax.random.normal(base_key, (count, span, HEADS, HEAD_DIM), jnp.float32)
    values = jnp.clip(values, -4.0, 4.0)
    return values.reshape(count, span, HEADS * HEAD_DIM)


def draw_self_len(key, part):
    return length_draw(jax.random.fold_in(key, 11), REQUESTS, S_MAX)


def draw_cross_len(key, part):
    return length_draw(jax.random.fold_in(key, 13), REQUESTS, E_MAX)


def draw_self_keys(key, part):
    return key_draw(jax.random.fold_in(key, 17), REQUESTS, S_MAX).astype(jnp.bfloat16)


def draw_cross_keys(key, part):
    return key_draw(jax.random.fold_in(key, 19), REQUESTS, E_MAX).astype(jnp.bfloat16)


def set_ends(array, key, smallest, top_value):
    extent = array.shape
    spot = [jax.random.randint(jax.random.fold_in(key, axis), (), 0, extent[axis]) for axis in range(len(extent))]
    array = array.at[tuple(spot)].set(smallest)
    longest = extent.index(max(extent))
    spot[longest] = (spot[longest] + 1) % extent[longest]
    return array.at[tuple(spot)].set(top_value)


def shard_levels(own_key, shape, shards, least, largest):
    level, own = 1.0, jax.random.fold_in(own_key, 6)
    for dim, parts in shards:
        heights = jnp.exp(jax.random.uniform(jax.random.fold_in(own, dim), (parts,), jnp.float32, least / len(shards), largest / len(shards)))
        level = level * jnp.repeat(heights, shape[dim] // parts).reshape([-1 if axis == dim else 1 for axis in range(len(shape))])
    return level


def scatter_about(stream_key, dims, width, reach, cuts=(), held_as=jnp.bfloat16):
    loudness = shard_levels(stream_key, dims, cuts, -0.22, 0.18) if cuts else 1.0
    entries = jax.random.normal(stream_key, dims, jnp.float32) * width * loudness
    return jnp.minimum(jnp.maximum(entries, -reach), reach).astype(held_as)


def setup_inputs(seed: int = 0) -> dict:
    key_list = jax.random.split(jax.random.key(seed), 20)
    tokens = scatter_about(key_list[0], (REQUESTS, D), 1.0, 6.0, ((0, 16),))
    self_keys = draw_self_keys(jax.random.fold_in(key_list[19], 71), 0)
    self_values = scatter_about(key_list[2], (REQUESTS, S_MAX, D), 1.0, 6.0, ((0, 16), (2, 2)))
    self_len = draw_self_len(jax.random.fold_in(key_list[19], 71), 0)
    cross_keys = draw_cross_keys(jax.random.fold_in(key_list[19], 71), 0)
    cross_values = scatter_about(key_list[5], (REQUESTS, E_MAX, D), 1.0, 6.0, ((0, 16), (2, 2)))
    cross_len = draw_cross_len(jax.random.fold_in(key_list[19], 71), 0)
    give_slot = set_ends(jax.random.randint(key_list[7], (MOVES,), 0, REQ_DEV), jax.random.fold_in(key_list[7], 1), 0, REQ_DEV - 1).astype(jnp.int32)
    w_query = scatter_about(key_list[8], (D, D), D ** -0.5, 0.1875, ((1, 2),))
    w_key = scatter_about(key_list[9], (D, D), D ** -0.5, 0.1875, ((1, 2),))
    w_value = scatter_about(key_list[10], (D, D), D ** -0.5, 0.1875, ((1, 2),))
    w_out = scatter_about(key_list[11], (D, D), D ** -0.5, 0.1875, ((0, 2),))
    w_cross_query = scatter_about(key_list[12], (D, D), D ** -0.5, 0.1875, ((1, 2),))
    w_cross_out = scatter_about(key_list[13], (D, D), D ** -0.5, 0.1875, ((0, 2),))
    w_up = scatter_about(key_list[14], (D, FF), D ** -0.5, 0.1875, ((1, 2),))
    w_down = scatter_about(key_list[15], (FF, D), FF ** -0.5, 0.09375, ((0, 2),))
    gain_self = jnp.clip(1.0 + 0.18 * jax.random.normal(key_list[16], (D,), jnp.float32), 0.1, 1.9)
    gain_cross = jnp.clip(1.0 + 0.18 * jax.random.normal(key_list[17], (D,), jnp.float32), 0.1, 1.9)
    gain_final = jnp.clip(1.0 + 0.18 * jax.random.normal(key_list[18], (D,), jnp.float32), 0.1, 1.9)
    return {"tokens": tokens, "self_keys": self_keys, "self_values": self_values, "self_len": self_len, "cross_keys": cross_keys, "cross_values": cross_values, "cross_len": cross_len, "give_slot": give_slot, "w_query": w_query, "w_key": w_key, "w_value": w_value, "w_out": w_out, "w_cross_query": w_cross_query, "w_cross_out": w_cross_out, "w_up": w_up, "w_down": w_down, "gain_self": gain_self, "gain_cross": gain_cross, "gain_final": gain_final}


def rounded(value):
    return lax.optimization_barrier(value.astype(jnp.bfloat16)).astype(jnp.float32)

def layer_norm(value, gain):
    mean = lax.optimization_barrier(jnp.mean(value, axis=-1, keepdims=True))
    centred = value - mean
    spread = lax.optimization_barrier(jnp.mean(centred * centred, axis=-1, keepdims=True))
    return centred * lax.rsqrt(spread + 1e-05) * gain

def project(left, right):
    return jnp.dot(left, right, preferred_element_type=jnp.float32)

def attend_fresh(inputs):
    query, keys, values, length, fresh_key, fresh_value = inputs
    qf = query.astype(jnp.float32)
    scores = jnp.einsum('hd,shd->hs', qf, keys.astype(jnp.float32))
    places = jnp.arange(keys.shape[0], dtype=jnp.int32)
    scores = jnp.where(places[None, :] < length, scores, -jnp.inf)
    own = lax.optimization_barrier(jnp.sum(qf * fresh_key.astype(jnp.float32), axis=1))
    top = jnp.maximum(lax.optimization_barrier(jnp.max(scores, axis=1)), own)
    weights = jnp.exp(scores - top[:, None])
    own_weight = jnp.exp(own - top)
    total = lax.optimization_barrier(jnp.sum(weights, axis=1)) + own_weight
    mixed = jnp.einsum('hs,shd->hd', rounded(weights), values.astype(jnp.float32))
    mixed = mixed + rounded(own_weight)[:, None] * fresh_value.astype(jnp.float32)
    return (mixed / total[:, None]).astype(jnp.bfloat16)

def attend_plain(inputs):
    query, keys, values, length = inputs
    scores = jnp.einsum('hd,shd->hs', query.astype(jnp.float32), keys.astype(jnp.float32))
    places = jnp.arange(keys.shape[0], dtype=jnp.int32)
    scores = jnp.where(places[None, :] < length, scores, -jnp.inf)
    top = lax.optimization_barrier(jnp.max(scores, axis=1))
    weights = jnp.exp(scores - top[:, None])
    total = lax.optimization_barrier(jnp.sum(weights, axis=1))
    mixed = jnp.einsum('hs,shd->hd', rounded(weights), values.astype(jnp.float32))
    return (mixed / total[:, None]).astype(jnp.bfloat16)

def reference(tokens, self_keys, self_values, self_len, cross_keys, cross_values, cross_len, give_slot, w_query, w_key, w_value, w_out, w_cross_query, w_cross_out, w_up, w_down, gain_self, gain_cross, gain_final):
    scale = HEAD_DIM ** (-0.5)
    count = tokens.shape[0]
    query = (project(tokens, w_query) * scale).astype(jnp.bfloat16)
    fresh_keys = project(tokens, w_key).astype(jnp.bfloat16)
    fresh_values = project(tokens, w_value).astype(jnp.bfloat16)
    heads = (count, HEADS, HEAD_DIM)
    self_mixed = lax.map(attend_fresh, (query.reshape(heads), self_keys.reshape(count, S_MAX, HEADS, HEAD_DIM), self_values.reshape(count, S_MAX, HEADS, HEAD_DIM), self_len, fresh_keys.reshape(heads), fresh_values.reshape(heads)))
    first = layer_norm(tokens.astype(jnp.float32) + project(self_mixed.reshape(count, D), w_out), gain_self).astype(jnp.bfloat16)
    cross_query = (project(first, w_cross_query) * scale).astype(jnp.bfloat16)
    cross_mixed = lax.map(attend_plain, (cross_query.reshape(heads), cross_keys.reshape(count, E_MAX, HEADS, HEAD_DIM), cross_values.reshape(count, E_MAX, HEADS, HEAD_DIM), cross_len))
    second = layer_norm(first.astype(jnp.float32) + project(cross_mixed.reshape(count, D), w_cross_out), gain_cross).astype(jnp.bfloat16)
    hidden = jax.nn.gelu(project(second, w_up), approximate=False).astype(jnp.bfloat16)
    layer_out = layer_norm(second.astype(jnp.float32) + project(hidden, w_down), gain_final).astype(jnp.bfloat16)
    index = jnp.arange(REQUESTS, dtype=jnp.int32)
    device = index // REQ_DEV
    slot_of = index % REQ_DEV
    partner = (device + MOVES // 2) % MOVES
    source = jnp.where(slot_of == give_slot[device], partner * REQ_DEV + give_slot[partner], index).astype(jnp.int32)
    decoded = layer_out[source]
    new_keys = fresh_keys[source]
    new_values = fresh_values[source]
    devices = jnp.arange(MOVES, dtype=jnp.int32)
    giver = (devices + MOVES // 2) % MOVES
    arrivals = (giver * REQ_DEV + give_slot[giver]).astype(jnp.int32)
    moved_keys = self_keys[arrivals]
    moved_values = self_values[arrivals]
    return (decoded, new_keys, new_values, moved_keys, moved_values)
```

```python
import jax
import jax.numpy as jnp
from jax import lax
from jax.sharding import PartitionSpec as P

HEAD_DIM = 64


def passed_along(block, axis, distance):
    devices = range(lax.axis_size(axis))
    route = [((i - distance) % len(devices), i) for i in devices]
    return lax.ppermute(block, axis, route)


def layer_norm(value, gain):
    mean = jnp.mean(value, axis=-1, keepdims=True)
    centred = value - mean
    spread = jnp.mean(centred * centred, axis=-1, keepdims=True)
    return centred * lax.rsqrt(spread + 1e-05) * gain


def attend(query, keys, values, lengths, fresh_key, fresh_value):
    count, span, width = keys.shape
    heads = width // HEAD_DIM
    block = min(512, span)
    query_heads = query.reshape(count, heads, HEAD_DIM)
    steps = (jnp.max(lengths) + block - 1) // block
    places = lax.iota(jnp.int32, block)

    def score_block(index, board):
        start = index * block
        piece = keys.reshape(count, block, heads, HEAD_DIM)
        scores = jnp.einsum("qhd,qshd->qhs", query_heads, piece, preferred_element_type=jnp.float32)
        valid = (start + places)[None, None, :] < lengths[:, None, None]
        scores = jnp.where(valid, scores, -jnp.inf)
        return scores

    board = lax.fori_loop(
        0, steps, score_block, jnp.full((count, heads, span), -jnp.inf, jnp.float32)
    )
    top = jnp.max(board, axis=2)
    if fresh_key is not None:
        own = jnp.sum(
            query_heads.astype(jnp.float32)
            * fresh_key.reshape(count, heads, HEAD_DIM).astype(jnp.float32),
            axis=2,
        )
        top = jnp.maximum(top, own)
    weights_all = jnp.exp(board - top[:, :, None])
    total = jnp.sum(weights_all, axis=2)

    def mix_block(index, accum):
        start = index * block
        weights = weights_all.astype(jnp.bfloat16)
        piece = values.reshape(count, block, heads, HEAD_DIM)
        return accum + jnp.einsum(
            "qhs,qshd->qhd", weights, piece, preferred_element_type=jnp.float32
        )

    mixed = lax.fori_loop(0, steps, mix_block, jnp.zeros((count, heads, HEAD_DIM), jnp.float32))
    if fresh_key is not None:
        own_weight = jnp.exp(own - top)
        total = total + own_weight
        mixed = mixed + own_weight.astype(jnp.bfloat16).astype(jnp.float32)[
            :, :, None
        ] * fresh_value.reshape(count, heads, HEAD_DIM).astype(jnp.float32)
    return (mixed / total[:, :, None]).astype(jnp.bfloat16).reshape(count, width)


def decode_layer(
    tokens, self_keys, self_values, self_len, cross_keys, cross_values, cross_len, params
):
    (
        w_query,
        w_key,
        w_value,
        w_out,
        w_cross_query,
        w_cross_out,
        w_up,
        w_down,
        gain_self,
        gain_cross,
        gain_final,
    ) = params
    scale = HEAD_DIM ** (-0.5)
    query = (jnp.dot(tokens, w_query, preferred_element_type=jnp.float32) * scale).astype(
        jnp.bfloat16
    )
    fresh_keys = jnp.dot(tokens, w_key, preferred_element_type=jnp.float32).astype(jnp.bfloat16)
    fresh_values = jnp.dot(tokens, w_value, preferred_element_type=jnp.float32).astype(jnp.bfloat16)
    self_mixed = attend(query, self_keys, self_values, self_len, fresh_keys, fresh_values)
    self_total = lax.psum(jnp.dot(self_mixed, w_out, preferred_element_type=jnp.float32), "head")
    first = layer_norm(tokens.astype(jnp.float32) + self_total, gain_self).astype(jnp.bfloat16)
    cross_query = (
        jnp.dot(first, w_cross_query, preferred_element_type=jnp.float32) * scale
    ).astype(jnp.bfloat16)
    cross_mixed = attend(cross_query, cross_keys, cross_values, cross_len, None, None)
    cross_total = lax.psum(
        jnp.dot(cross_mixed, w_cross_out, preferred_element_type=jnp.float32), "head"
    )
    second = layer_norm(first.astype(jnp.float32) + cross_total, gain_cross).astype(jnp.bfloat16)
    hidden = jax.nn.gelu(
        jnp.dot(second, w_up, preferred_element_type=jnp.float32), approximate=False
    ).astype(jnp.bfloat16)
    ffn_total = lax.psum(jnp.dot(hidden, w_down, preferred_element_type=jnp.float32), "head")
    layer_out = layer_norm(second.astype(jnp.float32) + ffn_total, gain_final).astype(jnp.bfloat16)
    return (layer_out, fresh_keys, fresh_values)


def take_slot(array, chosen):
    return lax.dynamic_slice_in_dim(array, chosen, 1, 0)


def put_slot(array, row, chosen):
    return lax.dynamic_update_slice_in_dim(array, row, chosen, 0)


def on_device(
    tokens,
    self_keys,
    self_values,
    self_len,
    cross_keys,
    cross_values,
    cross_len,
    give_slot,
    w_query,
    w_key,
    w_value,
    w_out,
    w_cross_query,
    w_cross_out,
    w_up,
    w_down,
    gain_self,
    gain_cross,
    gain_final,
):
    params = (
        w_query,
        w_key,
        w_value,
        w_out,
        w_cross_query,
        w_cross_out,
        w_up,
        w_down,
        gain_self,
        gain_cross,
        gain_final,
    )
    chosen = give_slot[0]
    half_axis = lax.axis_size("req") // 2
    moved_keys, moved_values = passed_along(
        (take_slot(self_keys, chosen), take_slot(self_values, chosen)), "req", half_axis
    )
    layer_out, fresh_keys, fresh_values = decode_layer(
        tokens, self_keys, self_values, self_len, cross_keys, cross_values, cross_len, params
    )
    rows = passed_along(
        (
            take_slot(layer_out, chosen),
            take_slot(fresh_keys, chosen),
            take_slot(fresh_values, chosen),
        ),
        "req",
        half_axis,
    )
    decoded = put_slot(layer_out, rows[0], chosen)
    new_keys = put_slot(fresh_keys, rows[1], chosen)
    new_values = put_slot(fresh_values, rows[2], chosen)
    return (decoded, new_keys, new_values, moved_keys, moved_values)


def solution(mesh):
    placed = (
        P("req", None),
        P("req", None, "head"),
        P("req", None, "head"),
        P("req"),
        P("req", None, "head"),
        P("req", None, "head"),
        P("req"),
        P("req"),
        P(None, "head"),
        P(None, "head"),
        P(None, "head"),
        P("head", None),
        P(None, "head"),
        P("head", None),
        P(None, "head"),
        P("head", None),
        P(),
        P(),
        P(),
    )
    return jax.shard_map(
        on_device,
        mesh=mesh,
        in_specs=placed,
        out_specs=(
            P("req", None),
            P("req", "head"),
            P("req", "head"),
            P("req", None, "head"),
            P("req", None, "head"),
        ),
        check_vma=False,
    )
```

```python
import functools

import jax
import jax.numpy as jnp
from jax import lax
from jax.experimental import pallas as pl
from jax.experimental.pallas import tpu as pltpu
from jax.sharding import PartitionSpec as P

HEAD_DIM = 64
LANES = 128
ROWS = 8
MESH = pl.DeviceIdType.MESH


def layer_norm(value, gain):
    mean = jnp.mean(value, axis=-1, keepdims=True)
    centred = value - mean
    spread = jnp.mean(centred * centred, axis=-1, keepdims=True)
    return centred * lax.rsqrt(spread + 1e-05) * gain


def rounded(value):
    return value.astype(jnp.bfloat16).astype(jnp.float32)


def project(left, right):
    return jnp.dot(left.astype(jnp.bfloat16), right, preferred_element_type=jnp.float32)


def attend_one(query, keys, values, length, fresh_key, fresh_value):
    width = query.shape[1]
    rows = max(ROWS, width // HEAD_DIM)
    head_of = lax.broadcasted_iota(jnp.int32, (rows, width), 1) // HEAD_DIM
    own_head = head_of == lax.broadcasted_iota(jnp.int32, (rows, width), 0)
    spread_query = jnp.where(own_head, query, 0.0)
    scores = lax.dot_general(
        spread_query.astype(jnp.bfloat16),
        keys,
        (((1,), (1,)), ((), ())),
        preferred_element_type=jnp.float32,
    )
    places = lax.broadcasted_iota(jnp.int32, scores.shape, 1)
    scores = jnp.where(places < length, scores, -jnp.inf)
    top = jnp.max(scores, axis=1, keepdims=True)
    if fresh_key is not None:
        own = jnp.sum(spread_query * fresh_key, axis=1, keepdims=True)
        top = jnp.maximum(top, own)
    weights = jnp.exp(scores - top)
    total = jnp.sum(weights, axis=1, keepdims=True)
    mixed = project(weights, values)
    if fresh_key is not None:
        own_weight = jnp.exp(own - top)
        total = total + own_weight
        mixed = mixed + rounded(own_weight) * fresh_value
    return jnp.sum(jnp.where(own_head, mixed / total, 0.0), axis=0, keepdims=True)


def kernel(
    parts,
    places,
    self_len,
    cross_len,
    give_slot,
    tokens,
    gain_self,
    gain_cross,
    gain_final,
    self_keys,
    self_values,
    cross_keys,
    cross_values,
    w_query,
    w_key,
    w_value,
    w_out,
    w_cross_query,
    w_cross_out,
    w_up,
    w_down,
    decoded,
    new_keys,
    new_values,
    moved_keys,
    moved_values,
    keys_in,
    values_in,
    cross_keys_in,
    cross_values_in,
    query_in,
    key_in,
    value_in,
    out_in,
    cross_query_in,
    cross_out_in,
    up_in,
    down_in,
    keys_away,
    values_away,
    hold,
    mix_hold,
    terms,
    row_away,
    row_home,
    load_sem,
    move_send,
    move_recv,
    term_send,
    term_recv,
):
    place = lax.axis_index("req")
    part = lax.axis_index("head")
    partner = lax.rem(place + places // 2, places)
    peers = [lax.rem(part + step, parts) for step in range(1, parts)]

    loads = []
    for index, (source, target) in enumerate(
        (
            (self_keys, keys_in),
            (self_values, values_in),
            (w_query, query_in),
            (w_key, key_in),
            (w_value, value_in),
            (w_out, out_in),
            (w_cross_query, cross_query_in),
            (cross_keys, cross_keys_in),
            (cross_values, cross_values_in),
            (w_cross_out, cross_out_in),
            (w_up, up_in),
            (w_down, down_in),
        )
    ):
        load = pltpu.make_async_copy(source, target, load_sem.at[index])
        load.start()
        loads.append(load)

    barrier = pltpu.get_barrier_semaphore()
    pl.semaphore_signal(barrier, inc=1, device_id=(partner, part), device_id_type=MESH)
    for peer in peers:
        pl.semaphore_signal(barrier, inc=1, device_id=(place, peer), device_id_type=MESH)

    chosen = give_slot[0]
    first_chosen = chosen == 0

    loads[0].wait()
    keys_away[...] = jnp.where(first_chosen, keys_in[0], keys_in[1])
    pl.semaphore_wait(barrier, parts)

    def send(source, target, index):
        copy = pltpu.make_async_remote_copy(
            src_ref=source,
            dst_ref=target,
            send_sem=move_send.at[index],
            recv_sem=move_recv.at[index],
            device_id=(partner, part),
            device_id_type=MESH,
        )
        copy.start()
        return copy

    keys_copy = send(keys_away, moved_keys.at[0], 0)
    loads[1].wait()
    values_away[...] = jnp.where(first_chosen, values_in[0], values_in[1])
    values_copy = send(values_away, moved_values.at[0], 1)

    def summed(phase, term):
        terms[phase, part] = term
        copies = []
        for step, peer in enumerate(peers):
            copy = pltpu.make_async_remote_copy(
                src_ref=terms.at[phase, part],
                dst_ref=terms.at[phase, part],
                send_sem=term_send.at[phase, step],
                recv_sem=term_recv.at[phase, step],
                device_id=(place, peer),
                device_id_type=MESH,
            )
            copy.start()
            copies.append(copy)
        for copy in copies:
            copy.wait()
        total = terms[phase, 0]
        for index in range(1, parts):
            total = total + terms[phase, index]
        return total

    count = tokens.shape[0]
    scale = HEAD_DIM ** (-0.5)
    hold[...] = jnp.zeros_like(hold)
    hold[0:count, :] = tokens[...].astype(jnp.float32)
    own = hold[...]
    loads[2].wait()
    query = rounded(project(own, query_in[...]) * scale)
    loads[3].wait()
    fresh_keys = rounded(project(own, key_in[...]))
    loads[4].wait()
    fresh_values = rounded(project(own, value_in[...]))

    mix_hold[...] = jnp.zeros_like(mix_hold)
    for index in range(count):
        mix_hold[index : index + 1, :] = attend_one(
            query[index : index + 1],
            keys_in[index],
            values_in[index],
            self_len[index],
            fresh_keys[index : index + 1],
            fresh_values[index : index + 1],
        )
    loads[5].wait()
    total = summed(0, project(mix_hold[...], out_in[...]))
    first = rounded(layer_norm(own + total, gain_self[...]))

    loads[6].wait()
    cross_query = rounded(project(first, cross_query_in[...]) * scale)
    loads[7].wait()
    loads[8].wait()
    for index in range(count):
        mix_hold[index : index + 1, :] = attend_one(
            cross_query[index : index + 1],
            cross_keys_in[index],
            cross_values_in[index],
            cross_len[index],
            None,
            None,
        )
    loads[9].wait()
    total = summed(1, project(mix_hold[...], cross_out_in[...]))
    second = rounded(layer_norm(first + total, gain_cross[...]))

    loads[10].wait()
    hidden = project(second, up_in[...])
    hidden = 0.5 * hidden * (1.0 + lax.erf(hidden * (0.5**0.5)))
    loads[11].wait()
    total = summed(2, project(hidden, down_in[...]))
    layer_out = rounded(layer_norm(second + total, gain_final[...]))

    results = ((layer_out, decoded), (fresh_keys, new_keys), (fresh_values, new_values))
    row_away[...] = jnp.zeros_like(row_away)
    spot = 0
    for value, _ in results:
        row = jnp.where(first_chosen, value[0:1], value[1:2])
        for piece in range(value.shape[1] // LANES):
            row_away[spot : spot + 1, :] = row[:, piece * LANES : (piece + 1) * LANES]
            spot += 1
    row_copy = send(row_away, row_home, 2)
    row_copy.wait()
    spot = 0
    for value, output in results:
        for piece in range(value.shape[1] // LANES):
            span = slice(piece * LANES, (piece + 1) * LANES)
            mine = value[0:count, span]
            slots = lax.broadcasted_iota(jnp.int32, mine.shape, 0)
            mine = jnp.where(slots == chosen, row_home[spot : spot + 1, :], mine)
            output[:, span] = mine.astype(jnp.bfloat16)
            spot += 1
    keys_copy.wait()
    values_copy.wait()


def on_device(
    tokens,
    self_keys,
    self_values,
    self_len,
    cross_keys,
    cross_values,
    cross_len,
    give_slot,
    w_query,
    w_key,
    w_value,
    w_out,
    w_cross_query,
    w_cross_out,
    w_up,
    w_down,
    gain_self,
    gain_cross,
    gain_final,
):
    parts, places = lax.axis_size("head"), lax.axis_size("req")
    count, depth = tokens.shape
    span, width = self_keys.shape[1:]
    pieces = (depth + 2 * width) // LANES
    tall = (pieces + ROWS - 1) // ROWS * ROWS
    big = (
        self_keys,
        self_values,
        cross_keys,
        cross_values,
        w_query,
        w_key,
        w_value,
        w_out,
        w_cross_query,
        w_cross_out,
        w_up,
        w_down,
    )
    whole = pl.BlockSpec(memory_space=pltpu.VMEM)
    scalars = pl.BlockSpec(memory_space=pltpu.SMEM)
    anywhere = pl.BlockSpec(memory_space=pl.ANY)
    bf16, f32 = jnp.bfloat16, jnp.float32
    size = sum(array.size for array in big)
    return pl.pallas_call(
        functools.partial(kernel, parts, places),
        out_shape=(
            jax.ShapeDtypeStruct((count, depth), bf16),
            jax.ShapeDtypeStruct((count, width), bf16),
            jax.ShapeDtypeStruct((count, width), bf16),
            jax.ShapeDtypeStruct((1, span, width), bf16),
            jax.ShapeDtypeStruct((1, span, width), bf16),
        ),
        in_specs=[scalars] * 3 + [whole] * 4 + [anywhere] * 12,
        out_specs=(whole, whole, whole, anywhere, anywhere),
        scratch_shapes=[pltpu.VMEM(array.shape, bf16) for array in big]
        + [
            pltpu.VMEM((span, width), bf16),
            pltpu.VMEM((span, width), bf16),
            pltpu.VMEM((ROWS, depth), f32),
            pltpu.VMEM((ROWS, width), f32),
            pltpu.VMEM((3, parts, ROWS, depth), f32),
            pltpu.VMEM((tall, LANES), f32),
            pltpu.VMEM((tall, LANES), f32),
            pltpu.SemaphoreType.DMA((len(big),)),
            pltpu.SemaphoreType.DMA((3,)),
            pltpu.SemaphoreType.DMA((3,)),
            pltpu.SemaphoreType.DMA((3, parts)),
            pltpu.SemaphoreType.DMA((3, parts)),
        ],
        compiler_params=pltpu.CompilerParams(
            collective_id=0, has_side_effects=True, vmem_limit_bytes=56 * 2**20
        ),
        cost_estimate=pl.CostEstimate(flops=4 * size, bytes_accessed=2 * size, transcendentals=0),
    )(
        self_len,
        cross_len,
        give_slot,
        tokens,
        gain_self.reshape(1, depth),
        gain_cross.reshape(1, depth),
        gain_final.reshape(1, depth),
        *big,
    )


def solution(mesh):
    placed = (
        P("req", None),
        P("req", None, "head"),
        P("req", None, "head"),
        P("req"),
        P("req", None, "head"),
        P("req", None, "head"),
        P("req"),
        P("req"),
        P(None, "head"),
        P(None, "head"),
        P(None, "head"),
        P("head", None),
        P(None, "head"),
        P("head", None),
        P(None, "head"),
        P("head", None),
        P(),
        P(),
        P(),
    )
    return jax.shard_map(
        on_device,
        mesh=mesh,
        in_specs=placed,
        out_specs=(
            P("req", None),
            P("req", "head"),
            P("req", "head"),
            P("req", None, "head"),
            P("req", None, "head"),
        ),
        check_vma=False,
    )
```

```python
import functools

import jax
import jax.numpy as jnp
from jax import lax
from jax.experimental import pallas as pl
from jax.experimental.pallas import tpu as pltpu
from jax.sharding import PartitionSpec as P

HEAD_DIM = 64
LANES = 128
ROWS = 8
MESH = pl.DeviceIdType.MESH


def layer_norm(value, gain):
    mean = jnp.mean(value, axis=-1, keepdims=True)
    centred = value - mean
    spread = jnp.mean(centred * centred, axis=-1, keepdims=True)
    return centred * lax.rsqrt(spread + 1e-05) * gain


def rounded(value):
    return value.astype(jnp.bfloat16).astype(jnp.float32)


def project(left, right):
    return jnp.dot(left.astype(jnp.bfloat16), right, preferred_element_type=jnp.float32)


def attend_one(query, keys, values, length, fresh_key, fresh_value):
    width = query.shape[1]
    rows = max(ROWS, width // HEAD_DIM)
    head_of = lax.broadcasted_iota(jnp.int32, (rows, width), 1) // HEAD_DIM
    own_head = head_of == lax.broadcasted_iota(jnp.int32, (rows, width), 0)
    spread_query = jnp.where(own_head, query, 0.0)
    scores = lax.dot_general(
        spread_query.astype(jnp.bfloat16),
        keys,
        (((1,), (1,)), ((), ())),
        preferred_element_type=jnp.float32,
    )
    places = lax.broadcasted_iota(jnp.int32, scores.shape, 1)
    scores = jnp.where(places < length, scores, -jnp.inf)
    top = jnp.max(scores, axis=1, keepdims=True)
    if fresh_key is not None:
        own = jnp.sum(spread_query * fresh_key, axis=1, keepdims=True)
        top = jnp.maximum(top, own)
    weights = jnp.exp(scores - top)
    total = jnp.sum(weights, axis=1, keepdims=True)
    mixed = project(weights, values)
    if fresh_key is not None:
        own_weight = jnp.exp(own - top)
        total = total + own_weight
        mixed = mixed + rounded(own_weight) * fresh_value
    return jnp.sum(jnp.where(own_head, mixed / total, 0.0), axis=0, keepdims=True)


def kernel(
    parts,
    places,
    self_len,
    cross_len,
    give_slot,
    tokens,
    gain_self,
    gain_cross,
    gain_final,
    self_keys,
    self_values,
    cross_keys,
    cross_values,
    w_query,
    w_key,
    w_value,
    w_out,
    w_cross_query,
    w_cross_out,
    w_up,
    w_down,
    decoded,
    new_keys,
    new_values,
    moved_keys,
    moved_values,
    keys_in,
    values_in,
    cross_keys_in,
    cross_values_in,
    query_in,
    key_in,
    value_in,
    out_in,
    cross_query_in,
    cross_out_in,
    up_in,
    down_in,
    keys_away,
    values_away,
    hold,
    mix_hold,
    terms,
    row_away,
    row_home,
    load_sem,
    move_send,
    move_recv,
    term_send,
    term_recv,
):
    place = lax.axis_index("req")
    part = lax.axis_index("head")
    partner = lax.rem(place + places // 2, places)
    peers = [lax.rem(part + step, parts) for step in range(1, parts)]

    loads = []
    for index, (source, target) in enumerate(
        (
            (self_keys, keys_in),
            (self_values, values_in),
            (w_query, query_in),
            (w_key, key_in),
            (w_value, value_in),
            (w_out, out_in),
            (w_cross_query, cross_query_in),
            (cross_keys, cross_keys_in),
            (cross_values, cross_values_in),
            (w_cross_out, cross_out_in),
            (w_up, up_in),
            (w_down, down_in),
        )
    ):
        load = pltpu.make_async_copy(source, target, load_sem.at[index])
        load.start()
        loads.append(load)

    barrier = pltpu.get_barrier_semaphore()
    pl.semaphore_signal(barrier, inc=1, device_id=(partner, part), device_id_type=MESH)
    for peer in peers:
        pl.semaphore_signal(barrier, inc=1, device_id=(place, peer), device_id_type=MESH)

    chosen = give_slot[0]
    first_chosen = chosen == 0

    loads[0].wait()
    keys_away[...] = jnp.where(first_chosen, keys_in[0], keys_in[1])
    pl.semaphore_wait(barrier, parts)

    def send(source, target, index):
        copy = pltpu.make_async_remote_copy(
            src_ref=source,
            dst_ref=target,
            send_sem=move_send.at[index],
            recv_sem=move_recv.at[index],
            device_id=(partner, part),
            device_id_type=MESH,
        )
        copy.start()
        return copy

    keys_copy = send(keys_away, moved_keys.at[0], 0)
    loads[1].wait()
    values_away[...] = jnp.where(first_chosen, values_in[0], values_in[1])
    values_copy = send(values_away, moved_values.at[0], 1)

    def summed(phase, term):
        terms[phase, part] = term
        copies = []
        for step, peer in enumerate(peers):
            copy = pltpu.make_async_remote_copy(
                src_ref=terms.at[phase, part],
                dst_ref=terms.at[phase, part],
                send_sem=term_send.at[phase, step],
                recv_sem=term_recv.at[phase, step],
                device_id=(place, peer),
                device_id_type=MESH,
            )
            copy.start()
            copies.append(copy)
        for copy in copies:
            copy.wait()
        total = terms[phase, 0]
        for index in range(1, parts):
            total = total + terms[phase, index]
        return total

    count = tokens.shape[0]
    scale = HEAD_DIM ** (-0.5)
    hold[...] = jnp.zeros_like(hold)
    hold[0:count, :] = tokens[...].astype(jnp.float32)
    own = hold[...]
    loads[2].wait()
    query = rounded(project(own, query_in[...]) * scale)
    loads[3].wait()
    fresh_keys = rounded(project(own, key_in[...]))
    loads[4].wait()
    fresh_values = rounded(project(own, value_in[...]))

    mix_hold[...] = jnp.zeros_like(mix_hold)
    for index in range(count):
        mix_hold[index : index + 1, :] = attend_one(
            query[index : index + 1],
            keys_in[index],
            values_in[index],
            self_len[index],
            fresh_keys[index : index + 1],
            fresh_values[index : index + 1],
        )
    loads[5].wait()
    total = summed(0, project(mix_hold[...], out_in[...]))
    first = rounded(layer_norm(own + total, gain_self[...]))

    loads[6].wait()
    cross_query = rounded(project(first, cross_query_in[...]) * scale)
    loads[7].wait()
    loads[8].wait()
    for index in range(count):
        mix_hold[index : index + 1, :] = attend_one(
            cross_query[index : index + 1],
            cross_keys_in[index],
            cross_values_in[index],
            cross_len[index],
            None,
            None,
        )
    loads[9].wait()
    total = summed(1, project(mix_hold[...], cross_out_in[...]))
    second = rounded(layer_norm(first + total, gain_cross[...]))

    loads[10].wait()
    hidden = project(second, up_in[...])
    hidden = 0.5 * hidden * (1.0 + lax.erf(hidden * (0.5**0.5)))
    loads[11].wait()
    total = summed(2, project(hidden, down_in[...]))
    layer_out = rounded(layer_norm(second + total, gain_final[...]))

    results = ((layer_out, decoded), (fresh_keys, new_keys), (fresh_values, new_values))
    row_away[...] = jnp.zeros_like(row_away)
    spot = 0
    for value, _ in results:
        row = jnp.where(first_chosen, value[0:1], value[1:2])
        for piece in range(value.shape[1] // LANES):
            row_away[spot : spot + 1, :] = row[:, piece * LANES : (piece + 1) * LANES]
            spot += 1
    row_copy = send(row_away, row_home, 2)
    row_copy.wait()
    spot = 0
    for value, output in results:
        for piece in range(value.shape[1] // LANES):
            span = slice(piece * LANES, (piece + 1) * LANES)
            mine = value[0:count, span]
            slots = lax.broadcasted_iota(jnp.int32, mine.shape, 0)
            mine = jnp.where(slots == chosen, row_home[spot : spot + 1, :], mine)
            output[:, span] = mine.astype(jnp.bfloat16)
            spot += 1
    keys_copy.wait()
    values_copy.wait()


def hand_over(*refs):
    count = (len(refs) - 1) // 2
    sems = refs[-1]
    order = sorted(range(count), key=lambda index: -refs[index].size)
    copies = [
        pltpu.make_async_copy(refs[index], refs[count + index], sems.at[index]) for index in order
    ]
    for copy in copies:
        copy.start()
    for copy in copies:
        copy.wait()


def on_device(
    tokens,
    self_keys,
    self_values,
    self_len,
    cross_keys,
    cross_values,
    cross_len,
    give_slot,
    w_query,
    w_key,
    w_value,
    w_out,
    w_cross_query,
    w_cross_out,
    w_up,
    w_down,
    gain_self,
    gain_cross,
    gain_final,
):
    parts, places = lax.axis_size("head"), lax.axis_size("req")
    count, depth = tokens.shape
    span, width = self_keys.shape[1:]
    pieces = (depth + 2 * width) // LANES
    tall = (pieces + ROWS - 1) // ROWS * ROWS
    big = (
        self_keys,
        self_values,
        cross_keys,
        cross_values,
        w_query,
        w_key,
        w_value,
        w_out,
        w_cross_query,
        w_cross_out,
        w_up,
        w_down,
    )
    whole = pl.BlockSpec(memory_space=pltpu.VMEM)
    scalars = pl.BlockSpec(memory_space=pltpu.SMEM)
    anywhere = pl.BlockSpec(memory_space=pl.ANY)
    bf16, f32 = jnp.bfloat16, jnp.float32
    size = sum(array.size for array in big)
    results = pl.pallas_call(
        functools.partial(kernel, parts, places),
        out_shape=(
            pltpu.VMEM((count, depth), bf16),
            pltpu.VMEM((count, width), bf16),
            pltpu.VMEM((count, width), bf16),
            pltpu.VMEM((1, span, width), bf16),
            pltpu.VMEM((1, span, width), bf16),
        ),
        in_specs=[scalars] * 3 + [whole] * 4 + [anywhere] * 12,
        out_specs=(whole,) * 5,
        scratch_shapes=[pltpu.VMEM(array.shape, bf16) for array in big]
        + [
            pltpu.VMEM((span, width), bf16),
            pltpu.VMEM((span, width), bf16),
            pltpu.VMEM((ROWS, depth), f32),
            pltpu.VMEM((ROWS, width), f32),
            pltpu.VMEM((3, parts, ROWS, depth), f32),
            pltpu.VMEM((tall, LANES), f32),
            pltpu.VMEM((tall, LANES), f32),
            pltpu.SemaphoreType.DMA((len(big),)),
            pltpu.SemaphoreType.DMA((3,)),
            pltpu.SemaphoreType.DMA((3,)),
            pltpu.SemaphoreType.DMA((3, parts)),
            pltpu.SemaphoreType.DMA((3, parts)),
        ],
        compiler_params=pltpu.CompilerParams(
            collective_id=0, has_side_effects=True, vmem_limit_bytes=58 * 2**20
        ),
        cost_estimate=pl.CostEstimate(flops=4 * size, bytes_accessed=2 * size, transcendentals=0),
    )(
        self_len,
        cross_len,
        give_slot,
        tokens,
        gain_self.reshape(1, depth),
        gain_cross.reshape(1, depth),
        gain_final.reshape(1, depth),
        *big,
    )
    return pl.pallas_call(
        hand_over,
        out_shape=tuple(jax.ShapeDtypeStruct(array.shape, array.dtype) for array in results),
        in_specs=[anywhere] * len(results),
        out_specs=(anywhere,) * len(results),
        scratch_shapes=[pltpu.SemaphoreType.DMA((len(results),))],
    )(*(pltpu.with_memory_space_constraint(array, pltpu.VMEM) for array in results))


def solution(mesh):
    placed = (
        P("req", None),
        P("req", None, "head"),
        P("req", None, "head"),
        P("req"),
        P("req", None, "head"),
        P("req", None, "head"),
        P("req"),
        P("req"),
        P(None, "head"),
        P(None, "head"),
        P(None, "head"),
        P("head", None),
        P(None, "head"),
        P("head", None),
        P(None, "head"),
        P("head", None),
        P(),
        P(),
        P(),
    )
    return jax.shard_map(
        on_device,
        mesh=mesh,
        in_specs=placed,
        out_specs=(
            P("req", None),
            P("req", "head"),
            P("req", "head"),
            P("req", None, "head"),
            P("req", None, "head"),
        ),
        check_vma=False,
    )
```

```python
import functools

import jax
import jax.numpy as jnp
from jax import lax
from jax.experimental import pallas as pl
from jax.experimental.pallas import tpu as pltpu
from jax.sharding import PartitionSpec as P

HEAD_DIM = 64
LANES = 128
ROWS = 8
MESH = pl.DeviceIdType.MESH


def layer_norm(value, gain):
    mean = jnp.mean(value, axis=-1, keepdims=True)
    centred = value - mean
    spread = jnp.mean(centred * centred, axis=-1, keepdims=True)
    return centred * lax.rsqrt(spread + 1e-05) * gain


def rounded(value):
    return value.astype(jnp.bfloat16).astype(jnp.float32)


def project(left, right):
    return jnp.dot(left.astype(jnp.bfloat16), right, preferred_element_type=jnp.float32)


def attend_one(query, keys, values, length, fresh_key, fresh_value):
    width = query.shape[1]
    rows = max(ROWS, width // HEAD_DIM)
    head_of = lax.broadcasted_iota(jnp.int32, (rows, width), 1) // HEAD_DIM
    own_head = head_of == lax.broadcasted_iota(jnp.int32, (rows, width), 0)
    spread_query = jnp.where(own_head, query, 0.0)
    scores = lax.dot_general(
        spread_query.astype(jnp.bfloat16),
        keys,
        (((1,), (1,)), ((), ())),
        preferred_element_type=jnp.float32,
    )
    places = lax.broadcasted_iota(jnp.int32, scores.shape, 1)
    scores = jnp.where(places < length, scores, -jnp.inf)
    top = jnp.max(scores, axis=1, keepdims=True)
    if fresh_key is not None:
        own = jnp.sum(spread_query * fresh_key, axis=1, keepdims=True)
        top = jnp.maximum(top, own)
    weights = jnp.exp(scores - top)
    total = jnp.sum(weights, axis=1, keepdims=True)
    mixed = project(weights, values)
    if fresh_key is not None:
        own_weight = jnp.exp(own - top)
        total = total + own_weight
        mixed = mixed + rounded(own_weight) * fresh_value
    return jnp.sum(jnp.where(own_head, mixed / total, 0.0), axis=0, keepdims=True)


def kernel(
    parts,
    places,
    self_len_out,
    cross_len_out,
    give_slot_out,
    tokens_out,
    gain_self_out,
    gain_cross_out,
    gain_final_out,
    self_keys,
    self_values,
    cross_keys,
    cross_values,
    w_query,
    w_key,
    w_value,
    w_out,
    w_cross_query,
    w_cross_out,
    w_up,
    w_down,
    decoded,
    new_keys,
    new_values,
    moved_keys,
    moved_values,
    keys_in,
    values_in,
    cross_keys_in,
    cross_values_in,
    query_in,
    key_in,
    value_in,
    out_in,
    cross_query_in,
    cross_out_in,
    up_in,
    down_in,
    self_len,
    cross_len,
    give_slot,
    tokens,
    gain_self,
    gain_cross,
    gain_final,
    keys_away,
    values_away,
    hold,
    mix_hold,
    terms,
    row_away,
    row_home,
    load_sem,
    move_send,
    move_recv,
    term_send,
    term_recv,
):
    place = lax.axis_index("req")
    part = lax.axis_index("head")
    partner = lax.rem(place + places // 2, places)
    peers = [lax.rem(part + step, parts) for step in range(1, parts)]

    barrier = pltpu.get_barrier_semaphore()
    pl.semaphore_signal(barrier, inc=1, device_id=(partner, part), device_id_type=MESH)
    for peer in peers:
        pl.semaphore_signal(barrier, inc=1, device_id=(place, peer), device_id_type=MESH)

    loads = []
    for index, (source, target) in enumerate(
        (
            (self_keys, keys_in),
            (self_values, values_in),
            (w_query, query_in),
            (w_key, key_in),
            (w_value, value_in),
            (w_out, out_in),
            (w_cross_query, cross_query_in),
            (cross_keys, cross_keys_in),
            (cross_values, cross_values_in),
            (w_cross_out, cross_out_in),
            (w_up, up_in),
            (w_down, down_in),
            (give_slot_out, give_slot),
            (tokens_out, tokens),
            (self_len_out, self_len),
            (cross_len_out, cross_len),
            (gain_self_out, gain_self),
            (gain_cross_out, gain_cross),
            (gain_final_out, gain_final),
        )
    ):
        load = pltpu.make_async_copy(source, target, load_sem.at[index])
        loads.append(load)
    for index in (0, 12, 1, 13, 2, 3, 4, 14, 5, 16, 6, 7, 15, 8, 9, 17, 10, 11, 18):
        loads[index].start()

    loads[12].wait()
    chosen = give_slot[0]
    first_chosen = chosen == 0

    loads[0].wait()
    keys_away[...] = jnp.where(first_chosen, keys_in[0], keys_in[1])
    pl.semaphore_wait(barrier, parts)

    def send(source, target, index):
        copy = pltpu.make_async_remote_copy(
            src_ref=source,
            dst_ref=target,
            send_sem=move_send.at[index],
            recv_sem=move_recv.at[index],
            device_id=(partner, part),
            device_id_type=MESH,
        )
        copy.start()
        return copy

    keys_copy = send(keys_away, moved_keys.at[0], 0)
    loads[1].wait()
    values_away[...] = jnp.where(first_chosen, values_in[0], values_in[1])
    values_copy = send(values_away, moved_values.at[0], 1)

    def summed(phase, term):
        terms[phase, part] = term
        copies = []
        for step, peer in enumerate(peers):
            copy = pltpu.make_async_remote_copy(
                src_ref=terms.at[phase, part],
                dst_ref=terms.at[phase, part],
                send_sem=term_send.at[phase, step],
                recv_sem=term_recv.at[phase, step],
                device_id=(place, peer),
                device_id_type=MESH,
            )
            copy.start()
            copies.append(copy)
        for copy in copies:
            copy.wait()
        total = terms[phase, 0]
        for index in range(1, parts):
            total = total + terms[phase, index]
        return total

    count = tokens.shape[0]
    scale = HEAD_DIM ** (-0.5)
    for index in range(13, 19):
        loads[index].wait()
    hold[...] = jnp.zeros_like(hold)
    hold[0:count, :] = tokens[...].astype(jnp.float32)
    own = hold[...]
    loads[2].wait()
    query = rounded(project(own, query_in[...]) * scale)
    loads[3].wait()
    fresh_keys = rounded(project(own, key_in[...]))
    loads[4].wait()
    fresh_values = rounded(project(own, value_in[...]))

    mix_hold[...] = jnp.zeros_like(mix_hold)
    for index in range(count):
        mix_hold[index : index + 1, :] = attend_one(
            query[index : index + 1],
            keys_in[index],
            values_in[index],
            self_len[index],
            fresh_keys[index : index + 1],
            fresh_values[index : index + 1],
        )
    loads[5].wait()
    total = summed(0, project(mix_hold[...], out_in[...]))
    first = rounded(layer_norm(own + total, gain_self[...]))

    loads[6].wait()
    cross_query = rounded(project(first, cross_query_in[...]) * scale)
    loads[7].wait()
    loads[8].wait()
    for index in range(count):
        mix_hold[index : index + 1, :] = attend_one(
            cross_query[index : index + 1],
            cross_keys_in[index],
            cross_values_in[index],
            cross_len[index],
            None,
            None,
        )
    loads[9].wait()
    total = summed(1, project(mix_hold[...], cross_out_in[...]))
    second = rounded(layer_norm(first + total, gain_cross[...]))

    loads[10].wait()
    hidden = project(second, up_in[...])
    hidden = 0.5 * hidden * (1.0 + lax.erf(hidden * (0.5**0.5)))
    loads[11].wait()
    total = summed(2, project(hidden, down_in[...]))
    layer_out = rounded(layer_norm(second + total, gain_final[...]))

    results = ((layer_out, decoded), (fresh_keys, new_keys), (fresh_values, new_values))
    row_away[...] = jnp.zeros_like(row_away)
    spot = 0
    for value, _ in results:
        row = jnp.where(first_chosen, value[0:1], value[1:2])
        for piece in range(value.shape[1] // LANES):
            row_away[spot : spot + 1, :] = row[:, piece * LANES : (piece + 1) * LANES]
            spot += 1
    row_copy = send(row_away, row_home, 2)
    row_copy.wait()
    spot = 0
    for value, output in results:
        for piece in range(value.shape[1] // LANES):
            span = slice(piece * LANES, (piece + 1) * LANES)
            mine = value[0:count, span]
            slots = lax.broadcasted_iota(jnp.int32, mine.shape, 0)
            mine = jnp.where(slots == chosen, row_home[spot : spot + 1, :], mine)
            output[:, span] = mine.astype(jnp.bfloat16)
            spot += 1
    keys_copy.wait()
    values_copy.wait()


def hand_over(*refs):
    count = (len(refs) - 1) // 2
    sems = refs[-1]
    order = sorted(range(count), key=lambda index: -refs[index].size)
    copies = [
        pltpu.make_async_copy(refs[index], refs[count + index], sems.at[index]) for index in order
    ]
    for copy in copies:
        copy.start()
    for copy in copies:
        copy.wait()


def on_device(
    tokens,
    self_keys,
    self_values,
    self_len,
    cross_keys,
    cross_values,
    cross_len,
    give_slot,
    w_query,
    w_key,
    w_value,
    w_out,
    w_cross_query,
    w_cross_out,
    w_up,
    w_down,
    gain_self,
    gain_cross,
    gain_final,
):
    parts, places = lax.axis_size("head"), lax.axis_size("req")
    count, depth = tokens.shape
    span, width = self_keys.shape[1:]
    pieces = (depth + 2 * width) // LANES
    tall = (pieces + ROWS - 1) // ROWS * ROWS
    big = (
        self_keys,
        self_values,
        cross_keys,
        cross_values,
        w_query,
        w_key,
        w_value,
        w_out,
        w_cross_query,
        w_cross_out,
        w_up,
        w_down,
    )
    whole = pl.BlockSpec(memory_space=pltpu.VMEM)
    anywhere = pl.BlockSpec(memory_space=pl.ANY)
    bf16, f32 = jnp.bfloat16, jnp.float32
    size = sum(array.size for array in big)
    results = pl.pallas_call(
        functools.partial(kernel, parts, places),
        out_shape=(
            pltpu.VMEM((count, depth), bf16),
            pltpu.VMEM((count, width), bf16),
            pltpu.VMEM((count, width), bf16),
            pltpu.VMEM((1, span, width), bf16),
            pltpu.VMEM((1, span, width), bf16),
        ),
        in_specs=[anywhere] * 19,
        out_specs=(whole,) * 5,
        scratch_shapes=[pltpu.VMEM(array.shape, bf16) for array in big]
        + [
            pltpu.SMEM(self_len.shape, self_len.dtype),
            pltpu.SMEM(cross_len.shape, cross_len.dtype),
            pltpu.SMEM(give_slot.shape, give_slot.dtype),
            pltpu.VMEM(tokens.shape, bf16),
            pltpu.VMEM((1, depth), f32),
            pltpu.VMEM((1, depth), f32),
            pltpu.VMEM((1, depth), f32),
            pltpu.VMEM((span, width), bf16),
            pltpu.VMEM((span, width), bf16),
            pltpu.VMEM((ROWS, depth), f32),
            pltpu.VMEM((ROWS, width), f32),
            pltpu.VMEM((3, parts, ROWS, depth), f32),
            pltpu.VMEM((tall, LANES), f32),
            pltpu.VMEM((tall, LANES), f32),
            pltpu.SemaphoreType.DMA((len(big) + 7,)),
            pltpu.SemaphoreType.DMA((3,)),
            pltpu.SemaphoreType.DMA((3,)),
            pltpu.SemaphoreType.DMA((3, parts)),
            pltpu.SemaphoreType.DMA((3, parts)),
        ],
        compiler_params=pltpu.CompilerParams(
            collective_id=0, has_side_effects=True, vmem_limit_bytes=58 * 2**20
        ),
        cost_estimate=pl.CostEstimate(flops=4 * size, bytes_accessed=2 * size, transcendentals=0),
    )(
        self_len,
        cross_len,
        give_slot,
        tokens,
        gain_self.reshape(1, depth),
        gain_cross.reshape(1, depth),
        gain_final.reshape(1, depth),
        *big,
    )
    return pl.pallas_call(
        hand_over,
        out_shape=tuple(jax.ShapeDtypeStruct(array.shape, array.dtype) for array in results),
        in_specs=[anywhere] * len(results),
        out_specs=(anywhere,) * len(results),
        scratch_shapes=[pltpu.SemaphoreType.DMA((len(results),))],
    )(*(pltpu.with_memory_space_constraint(array, pltpu.VMEM) for array in results))


def solution(mesh):
    placed = (
        P("req", None),
        P("req", None, "head"),
        P("req", None, "head"),
        P("req"),
        P("req", None, "head"),
        P("req", None, "head"),
        P("req"),
        P("req"),
        P(None, "head"),
        P(None, "head"),
        P(None, "head"),
        P("head", None),
        P(None, "head"),
        P("head", None),
        P(None, "head"),
        P("head", None),
        P(),
        P(),
        P(),
    )
    return jax.shard_map(
        on_device,
        mesh=mesh,
        in_specs=placed,
        out_specs=(
            P("req", None),
            P("req", "head"),
            P("req", "head"),
            P("req", None, "head"),
            P("req", None, "head"),
        ),
        check_vma=False,
    )
```
